256 devices in a mesh: store: 32 (over y, z), req: 4 (over x), tp: 2 (over core).
Axes of the slice: x: 4, y: 4, z: 8, core: 2. Of those that a mesh axis runs over, the one named last changes fastest.
Arguments:
- tokens: bfloat16 [16384, 8192], P(('store', 'req')), may hold values from -6 to 6
- queries: bfloat16 [16384, 8192], P(('store', 'req'), 'tp'), may hold values from -6 to 6
- plain_key_value: bfloat16 [16384, 2, 1024], P(('store', 'req'), None, 'tp'), may hold values from -6 to 6
- cached_key_value: bfloat16 [128, 2, 2048, 1024], P(('store', 'req'), None, None, 'tp'), may hold values from -6 to 6
- adapter_first_factor: bfloat16 [64, 8192, 128], P(None, ('store', 'tp')), may hold values from -0.0625 to 0.0625
- adapter_second_factor: bfloat16 [64, 2, 64, 1024], P('store', None, None, 'tp'), may hold values from -0.75 to 0.75
- request_adapter: int32 [128], P(('store', 'req')), may hold values from 0 to 63
- block_live_length: int32 [128], P(('store', 'req')), may hold values from 1 to 128, as said below
- context_length: int32 [128], P(('store', 'req')), may hold values from 0 to 2048, as said below
Outputs:
- new_kv: bfloat16 [16384, 2, 1024], P(('store', 'req'), None, 'tp')
- attention_out: bfloat16 [16384, 8192], P(('store', 'req'), 'tp')
The draws below stay inside these ranges and needn't reach their ends.
Inputs may be any that keep to these rules, and one draw needn't show every extreme that they name: `request_adapter`: each request's adapter. The first block_live_length rows of a block are live, the rest padding. The first context_length cached positions of a request are live.
All inputs are finite; a program needn't handle non-finite values.
Results may differ from the reference program's by a relative error of at most 0.0086.
Values may be sent and summed in bfloat16 or wider, within the bound.
A program may use at most 128 MiB of HBM per device.

```python
import math
import jax
import jax.numpy as jnp
import numpy as np
from jax import lax

MODEL_WIDTH = 8192
HEADS = 64
KEY_VALUE_HEADS = 8
HEAD_WIDTH = 128
ADAPTER_RANK = 64
BLOCK_LENGTH = 128
CTX = 2048
ADAPTER_TOTAL = 64
REQUESTS = 128
TOKENS = 16384


def draw_queries(key, part):
    key = jax.random.fold_in(key, 31)
    values = jnp.clip(jax.random.normal(key, (TOKENS, HEADS * HEAD_WIDTH), jnp.float32), -6.0, 6.0)
    return values.astype(jnp.bfloat16)


def draw_cached_key_value(key, part):
    key = jax.random.fold_in(key, 37)
    key_value_width = KEY_VALUE_HEADS * HEAD_WIDTH
    values = jnp.clip(jax.random.normal(key, (REQUESTS, 2, CTX, key_value_width), jnp.float32), -6.0, 6.0)
    return values.astype(jnp.bfloat16)


def draw_block_live_length(key, part):
    key = jax.random.fold_in(key, 11)
    lengths = jax.random.randint(key, (REQUESTS,), 1, BLOCK_LENGTH + 1)
    return lengths.at[0].set(BLOCK_LENGTH)


def draw_context_length(key, part):
    key = jax.random.fold_in(key, 23)
    lengths = jax.random.randint(key, (REQUESTS,), 0, CTX + 1)
    return lengths.at[REQUESTS - 1].set(CTX)


def with_ends(array, key, least, top_value):
    extent = array.shape
    spot = [jax.random.randint(jax.random.fold_in(key, axis), (), 0, extent[axis]) for axis in range(len(extent))]
    array = array.at[tuple(spot)].set(least)
    longest = extent.index(max(extent))
    spot[longest] = (spot[longest] + 1) % extent[longest]
    return array.at[tuple(spot)].set(top_value)


def shard_levels(rng, shape, shards, least, high):
    loudness = 1.0
    for position, shards_of in shards:
        draws = jax.random.uniform(jax.random.fold_in(jax.random.fold_in(rng, 6), position), (shards_of,), jnp.float32, least / len(shards), high / len(shards))
        loudness = loudness * jnp.repeat(jnp.exp(draws), shape[position] // shards_of).reshape((-1,) + (1,) * (len(shape) - 1 - position))
    return loudness


def rank_bounds(count, skew):
    portions = [(1 << 20) // math.isqrt(standing ** skew) + 1 for standing in range(1, count + 1)]
    spread = 1 + sum(portions) // (1 << 30)
    return np.cumsum(np.array([max(1, weight // spread) for weight in portions]))


def ranked(stream_key, extent, count, skew):
    table = rank_bounds(count, skew)
    ticket = jax.random.randint(jax.random.fold_in(stream_key, 1), extent, 0, int(table[count - 1]))
    standing = jnp.searchsorted(jnp.asarray(table, jnp.int32), ticket, side="right")
    return jax.random.permutation(jax.random.fold_in(stream_key, 2), count)[standing].astype(jnp.int32)


def normal_values(stream_key, dims, width, bound, split=(), held_as=jnp.bfloat16):
    drawn = jax.random.normal(stream_key, dims, jnp.float32) * width
    if len(split) > 0:
        drawn = shard_levels(stream_key, dims, split, -0.22, 0.18) * drawn
    return jnp.clip(drawn, min=-bound, max=bound).astype(held_as)


def setup_inputs(seed: int = 0) -> dict:
    splits = jax.random.split(jax.random.key(seed), 10)
    return {
        "tokens": normal_values(splits[0], (TOKENS, MODEL_WIDTH), 1.0, 6.0, ((0, 128),)),
        "queries": draw_queries(jax.random.fold_in(splits[9], 71), 0),
        "plain_key_value": normal_values(splits[2], (TOKENS, 2, KEY_VALUE_HEADS * HEAD_WIDTH), 1.0, 6.0, ((0, 128), (2, 2))),
        "cached_key_value": draw_cached_key_value(jax.random.fold_in(splits[9], 71), 0),
        "adapter_first_factor": normal_values(splits[4], (ADAPTER_TOTAL, MODEL_WIDTH, 2 * ADAPTER_RANK), MODEL_WIDTH ** -0.5, 0.0625, ((1, 64),)),
        "adapter_second_factor": normal_values(splits[5], (ADAPTER_TOTAL, 2, ADAPTER_RANK, KEY_VALUE_HEADS * HEAD_WIDTH), ADAPTER_RANK ** -0.5, 0.75, ((0, 32), (3, 2))),
        "request_adapter": with_ends(ranked(splits[6], (REQUESTS,), ADAPTER_TOTAL, 2), jax.random.fold_in(splits[6], 3), 0, ADAPTER_TOTAL - 1).astype(jnp.int32),
        "block_live_length": draw_block_live_length(jax.random.fold_in(splits[9], 71), 0),
        "context_length": draw_context_length(jax.random.fold_in(splits[9], 71), 0),
    }


def rotate_keys(key_heads, positions):
    half_size = key_heads.shape[-1] // 2
    index_float = jnp.arange(half_size).astype(jnp.float32)
    frequency = 10000.0 ** (-2.0 * index_float / key_heads.shape[-1])
    angles = positions.astype(jnp.float32)[:, None] * frequency[None, :]
    cosine = jnp.cos(angles)[:, None, :]
    sine_part = jnp.sin(angles)[:, None, :]
    first_half = key_heads[..., :half_size]
    second_half = key_heads[..., half_size:]
    return jnp.concatenate([first_half * cosine - second_half * sine_part, second_half * cosine + first_half * sine_part], axis=-1)

def attend_request(queries_r, cache_r, new_rows, live_rows, context_len):
    block_rows = queries_r.shape[0]
    key_value_width = new_rows.shape[-1]
    kv_heads = key_value_width // HEAD_WIDTH
    group_size = queries_r.shape[1] // key_value_width
    context = cache_r.shape[1]
    score_scale = 1.0 / math.sqrt(HEAD_WIDTH)
    query_rows = queries_r.astype(jnp.float32).reshape(block_rows, kv_heads, group_size, HEAD_WIDTH)
    keys_old = cache_r[0].astype(jnp.float32).reshape(context, kv_heads, HEAD_WIDTH)
    values_old = cache_r[1].astype(jnp.float32).reshape(context, kv_heads, HEAD_WIDTH)
    keys_new = new_rows[:, 0].astype(jnp.float32).reshape(block_rows, kv_heads, HEAD_WIDTH)
    values_new = new_rows[:, 1].astype(jnp.float32).reshape(block_rows, kv_heads, HEAD_WIDTH)
    score_old = jnp.einsum('ikgd,jkd->kgij', query_rows, keys_old) * score_scale
    score_new = jnp.einsum('ikgd,jkd->kgij', query_rows, keys_new) * score_scale
    positions = jnp.arange(block_rows)
    old_mask = jnp.arange(context) < context_len
    new_mask = (positions[None, :] <= positions[:, None]) & live_rows[None, :]
    score_old = jnp.where(old_mask[None, None, None, :], score_old, -jnp.inf)
    score_new = jnp.where(new_mask[None, None], score_new, -jnp.inf)
    highest = jnp.maximum(score_old.max(-1), score_new.max(-1))[..., None]
    exp_old = jnp.exp(score_old - highest)
    exp_new = jnp.exp(score_new - highest)
    denominator = exp_old.sum(-1, keepdims=True) + exp_new.sum(-1, keepdims=True)
    weight_old = lax.optimization_barrier((exp_old / denominator).astype(jnp.bfloat16)).astype(jnp.float32)
    weight_new = lax.optimization_barrier((exp_new / denominator).astype(jnp.bfloat16)).astype(jnp.float32)
    attended = jnp.einsum('kgij,jkd->ikgd', weight_old, values_old) + jnp.einsum('kgij,jkd->ikgd', weight_new, values_new)
    merged = attended.reshape(block_rows, -1)
    return jnp.where(live_rows[:, None], merged, 0.0).astype(jnp.bfloat16)

def reference(tokens, queries, plain_key_value, cached_key_value, adapter_first_factor, adapter_second_factor, request_adapter, block_live_length, context_length):
    key_value_width = KEY_VALUE_HEADS * HEAD_WIDTH
    request_data = (tokens.reshape(REQUESTS, BLOCK_LENGTH, MODEL_WIDTH), queries.reshape(REQUESTS, BLOCK_LENGTH, HEADS * HEAD_WIDTH), plain_key_value.reshape(REQUESTS, BLOCK_LENGTH, 2, key_value_width), cached_key_value, request_adapter, block_live_length, context_length)

    def one_request(request_items):
        token_rows_local, queries_r, plain_rows_local, cache_r, adapter_index, length, context_len = request_items
        rank_projection = jnp.dot(token_rows_local, adapter_first_factor[adapter_index], preferred_element_type=jnp.float32).astype(jnp.bfloat16)
        rank_projection = lax.optimization_barrier(rank_projection)
        adapter_update = jnp.einsum('zlo,lom->zlm', rank_projection.astype(jnp.float32).reshape(BLOCK_LENGTH, 2, ADAPTER_RANK), adapter_second_factor[adapter_index].astype(jnp.float32))
        updated_key_value = plain_rows_local.astype(jnp.float32) + adapter_update
        positions = jnp.arange(BLOCK_LENGTH)
        live_rows = positions < length
        rotated = rotate_keys(updated_key_value[:, 0].reshape(BLOCK_LENGTH, KEY_VALUE_HEADS, HEAD_WIDTH), context_len + positions).reshape(BLOCK_LENGTH, key_value_width)
        stacked = jnp.stack([rotated, updated_key_value[:, 1]], axis=1)
        new_rows = jnp.where(live_rows[:, None, None], stacked, 0.0).astype(jnp.bfloat16)
        attended = attend_request(queries_r, cache_r, new_rows, live_rows, context_len)
        return (new_rows, attended)
    new_kv, attention_out = lax.map(one_request, request_data)
    return (new_kv.reshape(TOKENS, 2, key_value_width), attention_out.reshape(TOKENS, HEADS * HEAD_WIDTH))
```

```python
import functools
import math

import jax
import jax.numpy as jnp
from jax import lax
from jax.experimental import pallas as pl
from jax.experimental.pallas import tpu as pltpu
from jax.sharding import PartitionSpec as P

HEAD = 128
ROWS = 128
RANK = 64
NY, NZ, NX = 4, 8, 4
PLANE = NY * NZ
GROUP = 8
KV_HEADS = 4
CTX = 2048
TILE = 512
SCALE2 = math.log2(math.e) / math.sqrt(HEAD)
LOWEST = -1e30
MESH = pl.DeviceIdType.MESH

OFFSETS = sorted(
    [(dy, dz) for dy in range(NY) for dz in range(NZ) if (dy, dz) != (0, 0)],
    key=lambda o: -(2 * min(o[1], NZ - o[1]) + min(o[0], NY - o[0])),
)


def slot(dy, dz):
    return (dy % NY) * NZ + dz % NZ


def kernel(
    adapter_ref, live_ref, ctx_ref, tokens, queries, plain, cached, first, second,
    new_out, attn_out,
    tok_v, q_v, plain_v, kv_v, first_v, send_a, recv_a, gath, send2, recv2, send3, recv3,
    part, part_in, key_buf, val_buf, acc, top, cos_v, sin_v, new_v, out_v, ids, xids,
    lsem, kvsem, osem, id_s, id_r, xid_s, xid_r, a_s, a_r, b1_s, b1_r, b2_s, b2_r, b3_s, b3_r, p_s, p_r,
):
    store, req, core = lax.axis_index("store"), lax.axis_index("req"), lax.axis_index("tp")
    y, z = store // NZ, lax.rem(store, NZ)

    def plane(dy, dz):
        return {"store": lax.rem(y + dy % NY, NY) * NZ + lax.rem(z + dz % NZ, NZ)}

    def across(dx):
        return {"req": lax.rem(req + dx % NX, NX)}

    sibling = {"tp": 1 - core}

    def remote(src, dst, s, r, dev):
        return pltpu.make_async_remote_copy(
            src_ref=src, dst_ref=dst, send_sem=s, recv_sem=r, device_id=dev, device_id_type=MESH
        )

    bar = pltpu.get_barrier_semaphore()
    peers = [plane(*o) for o in OFFSETS] + [across(dx) for dx in range(1, NX)] + [sibling]
    for dev in peers:
        pl.semaphore_signal(bar, inc=1, device_id=dev, device_id_type=MESH)

    def head_cols(h):
        return pl.ds(h * HEAD, HEAD)

    load_q = pltpu.make_async_copy(queries, q_v, lsem.at[0])
    load_q.start()
    load_kv = []
    for h in range(KV_HEADS):
        c = pltpu.make_async_copy(
            cached.at[0, :, :, head_cols(h)], kv_v.at[:, :, head_cols(h)], kvsem.at[h]
        )
        c.start()
        load_kv.append(c)
    load_b = pltpu.make_async_copy(
        second.at[:, :, pl.ds(pl.multiple_of(req * 16, 16), 16), :], gath.at[0], lsem.at[1]
    )
    load_b.start()
    load_a = pltpu.make_async_copy(first, first_v, lsem.at[2])
    load_a.start()
    load_p = pltpu.make_async_copy(plain, plain_v, lsem.at[3])
    load_p.start()
    load_t = pltpu.make_async_copy(tokens, tok_v, lsem.at[4])
    load_t.start()

    ctx = ctx_ref[0]
    live = live_ref[0]
    ids[0, 0] = adapter_ref[0]

    def attend(h):
        load_kv[h].wait()
        alive = lax.broadcasted_iota(jnp.int32, (CTX, HEAD), 0) < ctx
        k = kv_v[0, :, head_cols(h)]
        v = kv_v[1, :, head_cols(h)]
        key_buf[...] = jnp.where(alive, k, jnp.broadcast_to(k[0:1, :], k.shape))
        val_buf[:, 0:HEAD] = jnp.where(alive, v, jnp.zeros_like(v))
        val_buf[:, HEAD:] = jnp.where(alive, jnp.ones_like(v), jnp.zeros_like(v))
        per = TILE // ROWS
        for u in range(GROUP // per):
            g = h * GROUP + u * per
            q = jnp.concatenate([q_v[:, head_cols(g + i)] for i in range(per)], axis=0)
            s = lax.dot_general(
                q, key_buf[...], (((1,), (1,)), ((), ())), preferred_element_type=jnp.float32
            )
            m = jnp.max(s, axis=1, keepdims=True)
            p = jnp.exp2(s * SCALE2 - m * SCALE2).astype(jnp.bfloat16)
            r = pl.ds(g * ROWS, TILE)
            acc[r, :] = jnp.dot(p, val_buf[...], preferred_element_type=jnp.float32)
            m = jnp.where(ctx > 0, m, LOWEST)
            top[r, :] = jnp.broadcast_to(m, (TILE, HEAD))

    load_q.wait()
    attend(0)

    lane = lax.broadcasted_iota(jnp.int32, (ROWS, HEAD), 1)
    row = lax.broadcasted_iota(jnp.int32, (ROWS, HEAD), 0)
    index = jnp.where(lane < HEAD // 2, lane, lane - HEAD // 2).astype(jnp.float32)
    frequency = jnp.exp(index * (-2.0 / HEAD * math.log(10000.0)))
    angle = (ctx + row).astype(jnp.float32) * frequency
    cos_v[...] = jnp.cos(angle)
    sine = jnp.sin(angle)
    sin_v[...] = jnp.where(lane < HEAD // 2, -sine, sine)

    pl.semaphore_wait(bar, len(peers))

    id_copies = []
    for dy, dz in OFFSETS:
        k = slot(dy, dz)
        c = remote(adapter_ref, ids.at[k], id_s.at[k], id_r.at[k], plane(dy, dz))
        c.start()
        id_copies.append(c)
    load_b.wait()
    b1 = []
    for dz in sorted(range(1, NZ), key=lambda d: -min(d, NZ - d)):
        c = remote(gath.at[0], gath.at[dz], b1_s.at[dz], b1_r.at[dz], plane(0, dz))
        c.start()
        b1.append(c)

    attend(1)

    for c in id_copies:
        c.wait()
    xid_copies = []
    for dx in range(1, NX):
        c = remote(ids, xids.at[dx], xid_s.at[dx], xid_r.at[dx], across(dx))
        c.start()
        xid_copies.append(c)
    load_a.wait()
    a_copies = {}
    for dy, dz in OFFSETS:
        k = slot(dy, dz)
        send_a[k] = first_v[ids[slot(-dy, -dz), 0]]
        c = remote(send_a.at[k], recv_a.at[k], a_s.at[k], a_r.at[k], plane(dy, dz))
        c.start()
        a_copies[k] = c
    recv_a[0] = first_v[ids[0, 0]]

    attend(2)

    for c in xid_copies:
        c.wait()
    for c in b1:
        c.wait()

    def request_id(dx, k):
        return ids[k, 0] if dx == 0 else xids[dx, k, 0]

    b2 = []
    for dy in (2, 1, 3, 0):
        for dx in range(NX):
            a = request_id(dx, slot(-dy, 0))
            from_z = jnp.bitwise_and(jnp.right_shift(a, 1), NZ - 1)
            there = jnp.bitwise_and(z - from_z + NZ, NZ - 1)
            piece = gath[there, jnp.bitwise_and(a, 1)]
            if dy == 0:
                recv2[0, dx] = piece
            else:
                send2[dy, dx] = piece
        if dy:
            c = remote(send2.at[dy], recv2.at[dy], b2_s.at[dy], b2_r.at[dy], plane(dy, 0))
            c.start()
            b2.append(c)

    attend(3)

    for c in b2:
        c.wait()
    b3 = []
    for dx in (2, 1, 3, 0):
        a = request_id(dx, 0)
        from_y = jnp.bitwise_and(jnp.right_shift(a, 4), NY - 1)
        there = jnp.bitwise_and(y - from_y + NY, NY - 1)
        piece = recv2[there, dx]
        if dx == 0:
            recv3[0] = piece
        else:
            send3[dx] = piece
            c = remote(send3.at[dx], recv3.at[dx], b3_s.at[dx], b3_r.at[dx], across(-dx))
            c.start()
            b3.append(c)

    load_t.wait()

    def token_cols(dy, dz):
        owner = lax.rem(y - dy + NY, NY) * NZ + lax.rem(z - dz + NZ, NZ)
        return tok_v[:, pl.ds(pl.multiple_of((owner * 2 + core) * 128, 128), 128)]

    order = sorted([(dy, dz) for dy in range(NY) for dz in range(NZ)],
                   key=lambda o: (2 * min(o[1], NZ - o[1]) + min(o[0], NY - o[0])))
    total = jnp.zeros((ROWS, 2 * RANK), jnp.float32)
    for lo in range(0, PLANE, 4):
        some = order[lo:lo + 4]
        for o in some:
            if o != (0, 0):
                a_copies[slot(*o)].wait()
        left = jnp.concatenate([token_cols(*o) for o in some], axis=1)
        right = jnp.concatenate([recv_a[slot(*o)] for o in some], axis=0)
        total = total + jnp.dot(left, right, preferred_element_type=jnp.float32)
    part[...] = total
    swap = remote(part, part_in, p_s, p_r, sibling)
    swap.start()
    for c in b3:
        c.wait()
    load_p.wait()
    swap.wait()
    rank = (part[...] + part_in[...]).astype(jnp.bfloat16)

    alive = lax.broadcasted_iota(jnp.int32, (ROWS, HEAD), 0) < live
    for j in range(2):
        base = plain_v[:, j, :].astype(jnp.float32)
        whole = jnp.concatenate([recv3[jnp.bitwise_and(x - req + NX, NX - 1), j] for x in range(NX)], axis=0)
        delta = jnp.dot(rank[:, j * RANK:(j + 1) * RANK], whole, preferred_element_type=jnp.float32)
        fresh = base + delta
        for h in range(KV_HEADS):
            one = fresh[:, h * HEAD:(h + 1) * HEAD]
            if j == 0:
                one = one * cos_v[...] + pltpu.roll(one, HEAD // 2, 1) * sin_v[...]
            new_v[j, :, head_cols(h)] = jnp.where(alive, one, 0.0).astype(jnp.bfloat16)
    put_new = pltpu.make_async_copy(new_v, new_out, osem.at[KV_HEADS])
    put_new.start()

    column = lax.broadcasted_iota(jnp.int32, (ROWS, HEAD), 1)
    allowed = (column <= row) & (column < live)
    puts = []
    for h in range(KV_HEADS):
        kn = new_v[0, :, head_cols(h)]
        vn = jnp.concatenate([new_v[1, :, head_cols(h)], jnp.ones((ROWS, HEAD), jnp.bfloat16)], axis=1)
        q = jnp.concatenate([q_v[:, head_cols(h * GROUP + i)] for i in range(GROUP)], axis=0)
        s = lax.dot_general(q, kn, (((1,), (1,)), ((), ())), preferred_element_type=jnp.float32)
        s = jnp.where(allowed[None], s.reshape(GROUP, ROWS, HEAD), LOWEST).reshape(GROUP * ROWS, HEAD)
        r = pl.ds(h * GROUP * ROWS, GROUP * ROWS)
        old = top[r, :]
        m = jnp.maximum(jnp.max(s, axis=1, keepdims=True), old)
        p = jnp.exp2((s - m) * SCALE2).astype(jnp.bfloat16)
        o = jnp.dot(p, vn, preferred_element_type=jnp.float32)
        alpha = jnp.exp2((old - m) * SCALE2)
        top_part = acc[r, 0:HEAD] * alpha + o[:, 0:HEAD]
        bottom = acc[r, HEAD:] * alpha + o[:, HEAD:]
        res = top_part / bottom
        for g in range(GROUP):
            one = jnp.where(alive, res[g * ROWS:(g + 1) * ROWS, :], 0.0)
            out_v[:, head_cols(h * GROUP + g)] = one.astype(jnp.bfloat16)
        cols = pl.ds(h * GROUP * HEAD, GROUP * HEAD)
        c = pltpu.make_async_copy(out_v.at[:, cols], attn_out.at[:, cols], osem.at[h])
        c.start()
        puts.append(c)
    for c in puts:
        c.wait()
    put_new.wait()


def shards(tokens, queries, plain, cached, first, second, adapter, live, ctx):
    width = plain.shape[2]
    bf16, f32 = jnp.bfloat16, jnp.float32
    dma = pltpu.SemaphoreType.DMA
    smem = pl.BlockSpec(memory_space=pltpu.SMEM)
    hbm = pl.BlockSpec(memory_space=pl.ANY)
    heads = KV_HEADS * GROUP
    new, attn = pl.pallas_call(
        kernel,
        out_shape=(
            jax.ShapeDtypeStruct((2, ROWS, width), bf16),
            jax.ShapeDtypeStruct(queries.shape, bf16),
        ),
        in_specs=[smem] * 3 + [hbm] * 6,
        out_specs=(hbm, hbm),
        scratch_shapes=[
            pltpu.VMEM(tokens.shape, bf16),
            pltpu.VMEM(queries.shape, bf16),
            pltpu.VMEM(plain.shape, bf16),
            pltpu.VMEM((2, CTX, width), bf16),
            pltpu.VMEM(first.shape, bf16),
            pltpu.VMEM((PLANE, 128, 2 * RANK), bf16),
            pltpu.VMEM((PLANE, 128, 2 * RANK), bf16),
            pltpu.VMEM((NZ, 2, 2, 16, width), bf16),
            pltpu.VMEM((NY, NX, 2, 16, width), bf16),
            pltpu.VMEM((NY, NX, 2, 16, width), bf16),
            pltpu.VMEM((NX, 2, 16, width), bf16),
            pltpu.VMEM((NX, 2, 16, width), bf16),
            pltpu.VMEM((ROWS, 2 * RANK), f32),
            pltpu.VMEM((ROWS, 2 * RANK), f32),
            pltpu.VMEM((CTX, HEAD), bf16),
            pltpu.VMEM((CTX, 2 * HEAD), bf16),
            pltpu.VMEM((heads * ROWS, 2 * HEAD), f32),
            pltpu.VMEM((heads * ROWS, HEAD), f32),
            pltpu.VMEM((ROWS, HEAD), f32),
            pltpu.VMEM((ROWS, HEAD), f32),
            pltpu.VMEM((2, ROWS, width), bf16),
            pltpu.VMEM(queries.shape, bf16),
            pltpu.SMEM((PLANE, 1), jnp.int32),
            pltpu.SMEM((NX, PLANE, 1), jnp.int32),
            dma((5,)), dma((KV_HEADS,)), dma((KV_HEADS + 1,)),
            dma((PLANE,)), dma((PLANE,)), dma((NX,)), dma((NX,)),
            dma((PLANE,)), dma((PLANE,)), dma((NZ,)), dma((NZ,)),
            dma((NY,)), dma((NY,)), dma((NX,)), dma((NX,)), dma, dma,
        ],
        compiler_params=pltpu.CompilerParams(
            collective_id=0, has_side_effects=True, vmem_limit_bytes=58 << 20
        ),
    )(adapter, live, ctx, tokens, queries, plain, cached, first, second)
    return jnp.transpose(new, (1, 0, 2)), attn


def solution(mesh):
    in_specs = (
        P(("store", "req"), None),
        P(("store", "req"), "tp"),
        P(("store", "req"), None, "tp"),
        P(("store", "req"), None, None, "tp"),
        P(None, ("store", "tp"), None),
        P("store", None, None, "tp"),
        P(("store", "req")),
        P(("store", "req")),
        P(("store", "req")),
    )
    out_specs = (P(("store", "req"), None, "tp"), P(("store", "req"), "tp"))
    return jax.shard_map(shards, mesh=mesh, in_specs=in_specs, out_specs=out_specs, check_vma=False)
```

```python
import functools
import math

import jax
import jax.numpy as jnp
from jax import lax
from jax.experimental import pallas as pl
from jax.experimental.pallas import tpu as pltpu
from jax.sharding import PartitionSpec as P

HEAD = 128
ROWS = 128
RANK = 64
NY, NZ, NX = 4, 8, 4
PLANE = NY * NZ
GROUP = 8
KV_HEADS = 4
CTX = 2048
TILE = 512
SCALE2 = math.log2(math.e) / math.sqrt(HEAD)
LOWEST = -1e30
FAR_X = (2, 1, 3)
FAR_Y = (2, 1, 3)
FAR_Z = (4, 3, 5, 2, 6, 1, 7)
REST = (1, 7, 3, 5, 4, 0)
MESH = pl.DeviceIdType.MESH

def slot(dy, dz):
    return (dy % NY) * NZ + dz % NZ


def head_cols(h):
    return pl.ds(h * HEAD, HEAD)


def kernel(
    adapter_ref, live_ref, ctx_ref, tokens, queries, plain, cached, first, second,
    new_out, attn_out,
    tok_v, q_v, plain_v, base_v, kv_v, first_v, send_a, recv_a, gath, send2, recv2, send3, recv3,
    part, part_in, key_buf, val_buf, acc, top, angle_v, new_v, out_v, col, ids, xids,
    lsem, kvsem, osem, idy_s, idy_r, idz_s, idz_r, xid_s, xid_r, a_s, a_r,
    b1_s, b1_r, b2_s, b2_r, b3_s, b3_r, p_s, p_r,
):
    store, req, core = lax.axis_index("store"), lax.axis_index("req"), lax.axis_index("tp")
    y, z = store // NZ, lax.rem(store, NZ)

    def plane(dy, dz):
        return {"store": lax.rem(y + dy % NY, NY) * NZ + lax.rem(z + dz % NZ, NZ)}

    def across(dx):
        return {"req": lax.rem(req + dx % NX, NX)}

    sibling = {"tp": 1 - core}
    sends = []

    def remote(src, dst, s, r, dev):
        c = pltpu.make_async_remote_copy(
            src_ref=src, dst_ref=dst, send_sem=s, recv_sem=r, device_id=dev, device_id_type=MESH
        )
        c.start()
        sends.append(c)
        return c

    bar = pltpu.get_barrier_semaphore()
    peers = [plane(0, dz) for dz in FAR_Z] + [plane(dy, 0) for dy in FAR_Y]
    peers += [across(dx) for dx in FAR_X] + [sibling]
    for dev in peers:
        pl.semaphore_signal(bar, inc=1, device_id=dev, device_id_type=MESH)

    def load(src, dst, i):
        c = pltpu.make_async_copy(src, dst, lsem.at[i])
        c.start()
        return c

    load_q = load(queries, q_v, 0)
    load_kv = []
    for h in range(KV_HEADS):
        c = pltpu.make_async_copy(
            cached.at[0, :, :, head_cols(h)], kv_v.at[:, :, head_cols(h)], kvsem.at[h]
        )
        c.start()
        load_kv.append(c)
        if h == 0:
            load_b = load(second.at[:, :, pl.ds(pl.multiple_of(req * 16, 16), 16), :], gath.at[0], 1)
            load_p = load(plain, plain_v, 3)
            load_a = load(first, first_v, 2)
    load_t = load(tokens, tok_v, 4)

    ctx = ctx_ref[0]
    live = live_ref[0]
    col[0, 0] = adapter_ref[0]

    def attend(h, u):
        if u == 0:
            prepare(h)
        per = TILE // ROWS
        g = h * GROUP + u * per
        q = jnp.concatenate([q_v[:, head_cols(g + i)] for i in range(per)], axis=0)
        s = lax.dot_general(
            q, key_buf[...], (((1,), (1,)), ((), ())), preferred_element_type=jnp.float32
        )
        m = jnp.max(s, axis=1, keepdims=True) * SCALE2
        p = jnp.exp2(s * SCALE2 - m).astype(jnp.bfloat16)
        r = pl.ds(g * ROWS, TILE)
        acc[r, :] = jnp.dot(p, val_buf[...], preferred_element_type=jnp.float32)
        m = jnp.where(ctx > 0, m, LOWEST)
        top[r, :] = jnp.broadcast_to(m, (TILE, HEAD))

    def prepare(h):
        load_kv[h].wait()
        alive = lax.broadcasted_iota(jnp.int32, (CTX, HEAD), 0) < ctx
        k = kv_v[0, :, head_cols(h)]
        v = kv_v[1, :, head_cols(h)]
        key_buf[...] = jnp.where(alive, k, jnp.broadcast_to(k[0:1, :], k.shape))
        val_buf[:, 0:HEAD] = jnp.where(alive, v, jnp.zeros_like(v))
        val_buf[:, HEAD:] = jnp.where(alive, jnp.ones_like(v), jnp.zeros_like(v))

    load_q.wait()
    attend(0, 0)
    attend(0, 1)

    lane = lax.broadcasted_iota(jnp.int32, (ROWS, HEAD), 1)
    row = lax.broadcasted_iota(jnp.int32, (ROWS, HEAD), 0)
    index = jnp.where(lane < HEAD // 2, lane, lane - HEAD // 2).astype(jnp.float32)
    frequency = jnp.exp(index * (-2.0 / HEAD * math.log(10000.0)))
    angle = (ctx + row).astype(jnp.float32) * frequency
    angle_v[0] = jnp.cos(angle)
    sine = jnp.sin(angle)
    angle_v[1] = jnp.where(lane < HEAD // 2, -sine, sine)
    load_p.wait()
    for j in range(2):
        base_v[j] = plain_v[:, j, :]

    pl.semaphore_wait(bar, len(peers))

    id_y = {dy: remote(adapter_ref, col.at[dy], idy_s.at[dy], idy_r.at[dy], plane(dy, 0)) for dy in FAR_Y}
    load_b.wait()
    near = {}

    def pass_near(dz):
        near[dz] = remote(gath.at[0], gath.at[dz], b1_s.at[dz], b1_r.at[dz], plane(0, dz))

    def pass_on():
        for dz in (2, 6):
            near[dz].wait_recv()
        near[3] = remote(gath.at[2], gath.at[3], b1_s.at[3], b1_r.at[3], plane(0, 1))
        near[5] = remote(gath.at[6], gath.at[5], b1_s.at[5], b1_r.at[5], plane(0, -1))
        near[4] = remote(gath.at[2, 0], gath.at[4, 0], b1_s.at[4], b1_r.at[4], plane(0, 2))
        near[0] = remote(gath.at[6, 1], gath.at[4, 1], b1_s.at[0], b1_r.at[0], plane(0, -2))

    blocks = {}

    def send_block(dy, dz):
        k = slot(dy, dz)
        send_a[k] = first_v[col[-dy % NY, 0] if dz == 0 else ids[-dz % NZ, -dy % NY, 0]]
        blocks[k] = remote(send_a.at[k], recv_a.at[k], a_s.at[k], a_r.at[k], plane(dy, dz))

    def send_group(dz):
        if dz:
            id_z[-dz % NZ].wait_recv()
        else:
            recv_a[0] = first_v[col[0, 0]]
        for dy in FAR_Y + ((0,) if dz else ()):
            send_block(dy, dz)

    def request_id(dx, dy):
        return col[dy % NY, 0] if dx == 0 else xids[dx, dy % NY, 0]

    b2 = []

    def along_y():
        for c in id_x:
            c.wait_recv()
        for dz in REST:
            near[dz].wait_recv()
        for dy in FAR_Y + (0,):
            for dx in range(NX):
                a = request_id(dx, -dy)
                from_z = jnp.bitwise_and(jnp.right_shift(a, 1), NZ - 1)
                there = jnp.bitwise_and(z - from_z + NZ, NZ - 1)
                piece = gath[there, jnp.bitwise_and(a, 1)]
                if dy == 0:
                    recv2[0, dx] = piece
                else:
                    send2[dy, dx] = piece
            if dy:
                b2.append(remote(send2.at[dy], recv2.at[dy], b2_s.at[dy], b2_r.at[dy], plane(dy, 0)))

    b3 = []

    def along_x():
        for c in b2:
            c.wait_recv()
        for dx in FAR_X + (0,):
            a = request_id(dx, 0)
            from_y = jnp.bitwise_and(jnp.right_shift(a, 4), NY - 1)
            there = jnp.bitwise_and(y - from_y + NY, NY - 1)
            piece = recv2[there, dx]
            if dx == 0:
                recv3[0] = piece
            else:
                send3[dx] = piece
                b3.append(remote(send3.at[dx], recv3.at[dx], b3_s.at[dx], b3_r.at[dx], across(-dx)))

    for dz in (2, 6, 1, 7):
        pass_near(dz)
    attend(1, 0)
    for c in id_y.values():
        c.wait_recv()
    id_z = {dz: remote(col, ids.at[dz], idz_s.at[dz], idz_r.at[dz], plane(0, dz)) for dz in FAR_Z}
    id_x = [remote(col, xids.at[dx], xid_s.at[dx], xid_r.at[dx], across(dx)) for dx in FAR_X]
    attend(1, 1)
    load_a.wait()
    send_group(0)
    pass_on()
    send_group(4)
    send_group(3)
    send_group(5)
    send_group(2)
    send_group(6)
    send_group(1)
    send_group(7)
    along_y()
    attend(2, 0)
    attend(2, 1)
    along_x()
    attend(3, 0)
    attend(3, 1)

    load_t.wait()

    def token_cols(dy, dz):
        owner = lax.rem(y - dy + NY, NY) * NZ + lax.rem(z - dz + NZ, NZ)
        return tok_v[:, pl.ds(pl.multiple_of((owner * 2 + core) * 128, 128), 128)]

    total = jnp.zeros((ROWS, 2 * RANK), jnp.float32)
    for dz in (0,) + FAR_Z:
        some = [(dy, dz) for dy in FAR_Y + (0,)]
        for o in some:
            if o != (0, 0):
                blocks[slot(*o)].wait_recv()
        left = jnp.concatenate([token_cols(*o) for o in some], axis=1)
        right = jnp.concatenate([recv_a[slot(*o)] for o in some], axis=0)
        total = total + jnp.dot(left, right, preferred_element_type=jnp.float32)
    part[...] = total
    swap = remote(part, part_in, p_s, p_r, sibling)
    for c in b3:
        c.wait_recv()
    swap.wait_recv()
    rank = (part[...] + part_in[...]).astype(jnp.bfloat16)

    alive = lax.broadcasted_iota(jnp.int32, (ROWS, HEAD), 0) < live
    for j in range(2):
        whole = jnp.concatenate([recv3[jnp.bitwise_and(x - req + NX, NX - 1), j] for x in range(NX)], axis=0)
        delta = jnp.dot(rank[:, j * RANK:(j + 1) * RANK], whole, preferred_element_type=jnp.float32)
        fresh = base_v[j].astype(jnp.float32) + delta
        for h in range(KV_HEADS):
            one = fresh[:, h * HEAD:(h + 1) * HEAD]
            if j == 0:
                one = one * angle_v[0] + pltpu.roll(one, HEAD // 2, 1) * angle_v[1]
            new_v[j, :, head_cols(h)] = jnp.where(alive, one, 0.0).astype(jnp.bfloat16)
    puts = [pltpu.make_async_copy(new_v, new_out, osem.at[KV_HEADS])]
    puts[0].start()

    column = lax.broadcasted_iota(jnp.int32, (ROWS, HEAD), 1)
    allowed = (column <= row) & (column < live)
    for h in range(KV_HEADS):
        kn = new_v[0, :, head_cols(h)]
        vn = jnp.concatenate([new_v[1, :, head_cols(h)], jnp.ones((ROWS, HEAD), jnp.bfloat16)], axis=1)
        q = jnp.concatenate([q_v[:, head_cols(h * GROUP + i)] for i in range(GROUP)], axis=0)
        s = lax.dot_general(q, kn, (((1,), (1,)), ((), ())), preferred_element_type=jnp.float32)
        s = jnp.where(allowed[None], s.reshape(GROUP, ROWS, HEAD) * SCALE2, LOWEST)
        s = s.reshape(GROUP * ROWS, HEAD)
        r = pl.ds(h * GROUP * ROWS, GROUP * ROWS)
        old = top[r, :]
        m = jnp.maximum(jnp.max(s, axis=1, keepdims=True), old)
        p = jnp.exp2(s - m).astype(jnp.bfloat16)
        o = jnp.dot(p, vn, preferred_element_type=jnp.float32)
        alpha = jnp.exp2(old - m)
        upper = acc[r, 0:HEAD] * alpha + o[:, 0:HEAD]
        lower = acc[r, HEAD:] * alpha + o[:, HEAD:]
        res = upper / lower
        for g in range(GROUP):
            one = jnp.where(alive, res[g * ROWS:(g + 1) * ROWS, :], 0.0)
            out_v[:, head_cols(h * GROUP + g)] = one.astype(jnp.bfloat16)
        cols = pl.ds(h * GROUP * HEAD, GROUP * HEAD)
        c = pltpu.make_async_copy(out_v.at[:, cols], attn_out.at[:, cols], osem.at[h])
        c.start()
        puts.append(c)
    for c in sends:
        c.wait_send()
    for c in puts:
        c.wait()


def write_out(new, attn, new_out, attn_out, new_v, both_v, attn_v, sem, osem):
    loads = [pltpu.make_async_copy(new, new_v, sem.at[KV_HEADS])]
    for h in range(KV_HEADS):
        cols = pl.ds(h * GROUP * HEAD, GROUP * HEAD)
        loads.append(pltpu.make_async_copy(attn.at[:, cols], attn_v.at[:, cols], sem.at[h]))
    for c in loads:
        c.start()
    loads[0].wait()
    both_v[...] = jnp.stack([new_v[0], new_v[1]], axis=1)
    puts = [pltpu.make_async_copy(both_v, new_out, osem.at[KV_HEADS])]
    puts[0].start()
    for h in range(KV_HEADS):
        cols = pl.ds(h * GROUP * HEAD, GROUP * HEAD)
        loads[h + 1].wait()
        puts.append(pltpu.make_async_copy(attn_v.at[:, cols], attn_out.at[:, cols], osem.at[h]))
        puts[-1].start()
    for c in puts:
        c.wait()


def shards(tokens, queries, plain, cached, first, second, adapter, live, ctx):
    width = plain.shape[2]
    bf16, f32 = jnp.bfloat16, jnp.float32
    dma = pltpu.SemaphoreType.DMA
    smem = pl.BlockSpec(memory_space=pltpu.SMEM)
    hbm = pl.BlockSpec(memory_space=pl.ANY)
    heads = KV_HEADS * GROUP
    two = (2, ROWS, width)
    new, attn = pl.pallas_call(
        kernel,
        out_shape=(jax.ShapeDtypeStruct(two, bf16), jax.ShapeDtypeStruct(queries.shape, bf16)),
        in_specs=[smem] * 3 + [hbm] * 6,
        out_specs=(hbm, hbm),
        scratch_shapes=[
            pltpu.VMEM(tokens.shape, bf16),
            pltpu.VMEM(queries.shape, bf16),
            pltpu.VMEM(plain.shape, bf16),
            pltpu.VMEM(two, bf16),
            pltpu.VMEM((2, CTX, width), bf16),
            pltpu.VMEM(first.shape, bf16),
            pltpu.VMEM((PLANE, 128, 2 * RANK), bf16),
            pltpu.VMEM((PLANE, 128, 2 * RANK), bf16),
            pltpu.VMEM((NZ, 2, 2, 16, width), bf16),
            pltpu.VMEM((NY, NX, 2, 16, width), bf16),
            pltpu.VMEM((NY, NX, 2, 16, width), bf16),
            pltpu.VMEM((NX, 2, 16, width), bf16),
            pltpu.VMEM((NX, 2, 16, width), bf16),
            pltpu.VMEM((ROWS, 2 * RANK), f32),
            pltpu.VMEM((ROWS, 2 * RANK), f32),
            pltpu.VMEM((CTX, HEAD), bf16),
            pltpu.VMEM((CTX, 2 * HEAD), bf16),
            pltpu.VMEM((heads * ROWS, 2 * HEAD), f32),
            pltpu.VMEM((heads * ROWS, HEAD), f32),
            pltpu.VMEM((2, ROWS, HEAD), f32),
            pltpu.VMEM(two, bf16),
            pltpu.VMEM(queries.shape, bf16),
            pltpu.SMEM((PLANE, 1), jnp.int32),
            pltpu.SMEM((NZ, PLANE, 1), jnp.int32),
            pltpu.SMEM((NX, PLANE, 1), jnp.int32),
            dma((5,)), dma((KV_HEADS,)), dma((KV_HEADS + 1,)),
            dma((NY,)), dma((NY,)), dma((NZ,)), dma((NZ,)), dma((NX,)), dma((NX,)),
            dma((PLANE,)), dma((PLANE,)), dma((NZ,)), dma((NZ,)),
            dma((NY,)), dma((NY,)), dma((NX,)), dma((NX,)), dma, dma,
        ],
        compiler_params=pltpu.CompilerParams(
            collective_id=0, has_side_effects=True, vmem_limit_bytes=58 << 20
        ),
    )(adapter, live, ctx, tokens, queries, plain, cached, first, second)
    return pl.pallas_call(
        write_out,
        out_shape=(jax.ShapeDtypeStruct(plain.shape, bf16), jax.ShapeDtypeStruct(queries.shape, bf16)),
        in_specs=[hbm, hbm],
        out_specs=(hbm, hbm),
        scratch_shapes=[
            pltpu.VMEM(two, bf16),
            pltpu.VMEM(plain.shape, bf16),
            pltpu.VMEM(queries.shape, bf16),
            dma((KV_HEADS + 1,)),
            dma((KV_HEADS + 1,)),
        ],
        compiler_params=pltpu.CompilerParams(vmem_limit_bytes=58 << 20),
    )(new, attn)


def solution(mesh):
    in_specs = (
        P(("store", "req"), None),
        P(("store", "req"), "tp"),
        P(("store", "req"), None, "tp"),
        P(("store", "req"), None, None, "tp"),
        P(None, ("store", "tp"), None),
        P("store", None, None, "tp"),
        P(("store", "req")),
        P(("store", "req")),
        P(("store", "req")),
    )
    out_specs = (P(("store", "req"), None, "tp"), P(("store", "req"), "tp"))
    return jax.shard_map(shards, mesh=mesh, in_specs=in_specs, out_specs=out_specs, check_vma=False)
```

```python
import functools
import math

import jax
import jax.numpy as jnp
from jax import lax
from jax.experimental import pallas as pl
from jax.experimental.pallas import tpu as pltpu
from jax.sharding import PartitionSpec as P

HEAD = 128
ROWS = 128
RANK = 64
NY, NZ, NX = 4, 8, 4
PLANE = NY * NZ
GROUP = 8
KV_HEADS = 4
PIECE = 512
CTX = 2048
TILE = 512
SCALE2 = math.log2(math.e) / math.sqrt(HEAD)
LOWEST = -1e30
FAR_X = (2, 1, 3)
FAR_Y = (2, 1, 3)
FAR_Z = (4, 3, 5, 2, 6, 1, 7)
REST = (1, 7, 3, 5, 4, 0)
MESH = pl.DeviceIdType.MESH

def slot(dy, dz):
    return (dy % NY) * NZ + dz % NZ


def head_cols(h):
    return pl.ds(h * HEAD if isinstance(h, int) else pl.multiple_of(h * HEAD, HEAD), HEAD)


def kernel(
    adapter_ref, live_ref, ctx_ref, tokens, queries, plain, cached, first, second,
    new_k, new_w, o0, o1, o2, o3, o4, o5, o6, o7,
    tok_v, q_v, plain_v, base_v, kv_v, first_v, send_a, recv_a, gath, send2, recv2, send3, recv3,
    part, part_in, key_buf, val_buf, acc, top, angle_v, new_v, col, ids, xids,
    lsem, kvsem, idy_s, idy_r, idz_s, idz_r, xid_s, xid_r, a_s, a_r,
    b1_s, b1_r, b2_s, b2_r, b3_s, b3_r, p_s, p_r,
):
    store, req, core = lax.axis_index("store"), lax.axis_index("req"), lax.axis_index("tp")
    y, z = store // NZ, lax.rem(store, NZ)

    def plane(dy, dz):
        return {"store": lax.rem(y + dy % NY, NY) * NZ + lax.rem(z + dz % NZ, NZ)}

    def across(dx):
        return {"req": lax.rem(req + dx % NX, NX)}

    sibling = {"tp": 1 - core}
    sends = []

    def remote(src, dst, s, r, dev):
        c = pltpu.make_async_remote_copy(
            src_ref=src, dst_ref=dst, send_sem=s, recv_sem=r, device_id=dev, device_id_type=MESH
        )
        c.start()
        sends.append(c)
        return c

    bar = pltpu.get_barrier_semaphore()
    peers = [plane(0, dz) for dz in FAR_Z] + [plane(dy, 0) for dy in FAR_Y]
    peers += [across(dx) for dx in FAR_X] + [sibling]
    for dev in peers:
        pl.semaphore_signal(bar, inc=1, device_id=dev, device_id_type=MESH)

    def load(src, dst, i):
        c = pltpu.make_async_copy(src, dst, lsem.at[i])
        c.start()
        return c

    load_q = load(queries, q_v, 0)
    load_kv = []
    for h in range(KV_HEADS):
        c = pltpu.make_async_copy(
            cached.at[0, :, :, head_cols(h)], kv_v.at[:, :, head_cols(h)], kvsem.at[h]
        )
        c.start()
        load_kv.append(c)
        if h == 0:
            load_b = load(second.at[:, :, pl.ds(pl.multiple_of(req * 16, 16), 16), :], gath.at[0], 1)
            load_p = load(plain, plain_v, 3)
            load_a = load(first, first_v, 2)
    load_t = load(tokens, tok_v, 4)

    ctx = ctx_ref[0]
    live = live_ref[0]
    col[0, 0] = adapter_ref[0]

    def attend(h, u):
        per = TILE // ROWS
        g = h * GROUP + u * per
        q = jnp.concatenate([q_v[:, head_cols(g + i)] for i in range(per)], axis=0)
        s = lax.dot_general(
            q, key_buf[...], (((1,), (1,)), ((), ())), preferred_element_type=jnp.float32
        )
        m = jnp.max(s, axis=1, keepdims=True) * SCALE2
        p = jnp.exp2(s * SCALE2 - m).astype(jnp.bfloat16)
        o = jnp.dot(p, val_buf[...], preferred_element_type=jnp.float32)
        lower = jnp.where(ctx > 0, o[:, HEAD:], 1.0)
        r = pl.ds(pl.multiple_of(g * ROWS, ROWS), TILE)
        acc[r, :] = o[:, 0:HEAD] / lower
        top[r, :] = jnp.where(ctx > 0, m + jnp.log2(lower), LOWEST)

    def prepare(h):
        alive = lax.broadcasted_iota(jnp.int32, (CTX, HEAD), 0) < ctx
        k = kv_v[0, :, head_cols(h)]
        v = kv_v[1, :, head_cols(h)]
        key_buf[...] = jnp.where(alive, k, jnp.broadcast_to(k[0:1, :], k.shape))
        val_buf[:, 0:HEAD] = jnp.where(alive, v, jnp.zeros_like(v))
        val_buf[:, HEAD:] = jnp.where(alive, jnp.ones_like(v), jnp.zeros_like(v))

    lane = lax.broadcasted_iota(jnp.int32, (ROWS, HEAD), 1)
    row = lax.broadcasted_iota(jnp.int32, (ROWS, HEAD), 0)

    def attend_heads(lo, hi):
        for c in load_kv[lo:hi]:
            c.wait()

        @pl.loop(lo, hi)
        def _(h):
            prepare(h)
            for u in range(GROUP * ROWS // TILE):
                attend(h, u)

    def angles():
        index = jnp.where(lane < HEAD // 2, lane, lane - HEAD // 2).astype(jnp.float32)
        frequency = jnp.exp(index * (-2.0 / HEAD * math.log(10000.0)))
        angle = (ctx + row).astype(jnp.float32) * frequency
        angle_v[0] = jnp.cos(angle)
        sine = jnp.sin(angle)
        angle_v[1] = jnp.where(lane < HEAD // 2, -sine, sine)
        load_p.wait()
        for j in range(2):
            base_v[j] = plain_v[:, j, :]

    pl.semaphore_wait(bar, len(peers))

    id_y = {dy: remote(adapter_ref, col.at[dy], idy_s.at[dy], idy_r.at[dy], plane(dy, 0)) for dy in FAR_Y}
    load_b.wait()
    near = {}

    def pass_near(dz):
        near[dz] = remote(gath.at[0], gath.at[dz], b1_s.at[dz], b1_r.at[dz], plane(0, dz))

    def pass_on():
        for dz in (2, 6):
            near[dz].wait_recv()
        near[3] = remote(gath.at[2], gath.at[3], b1_s.at[3], b1_r.at[3], plane(0, 1))
        near[5] = remote(gath.at[6], gath.at[5], b1_s.at[5], b1_r.at[5], plane(0, -1))
        near[4] = remote(gath.at[2, 0], gath.at[4, 0], b1_s.at[4], b1_r.at[4], plane(0, 2))
        near[0] = remote(gath.at[6, 1], gath.at[4, 1], b1_s.at[0], b1_r.at[0], plane(0, -2))

    blocks = {}

    def send_block(dy, dz):
        k = slot(dy, dz)
        send_a[k] = first_v[col[-dy % NY, 0] if dz == 0 else ids[-dz % NZ, -dy % NY, 0]]
        blocks[k] = remote(send_a.at[k], recv_a.at[k], a_s.at[k], a_r.at[k], plane(dy, dz))

    def send_group(dz):
        if dz:
            id_z[-dz % NZ].wait_recv()
        else:
            recv_a[0] = first_v[col[0, 0]]
        for dy in FAR_Y + ((0,) if dz else ()):
            send_block(dy, dz)

    def request_id(dx, dy):
        return col[dy % NY, 0] if dx == 0 else xids[dx, dy % NY, 0]

    b2 = []

    def along_y():
        for c in id_x:
            c.wait_recv()
        for dz in REST:
            near[dz].wait_recv()
        for dy in FAR_Y + (0,):
            for dx in range(NX):
                a = request_id(dx, -dy)
                from_z = jnp.bitwise_and(jnp.right_shift(a, 1), NZ - 1)
                there = jnp.bitwise_and(z - from_z + NZ, NZ - 1)
                piece = gath[there, jnp.bitwise_and(a, 1)]
                if dy == 0:
                    recv2[0, dx] = piece
                else:
                    send2[dy, dx] = piece
            if dy:
                b2.append(remote(send2.at[dy], recv2.at[dy], b2_s.at[dy], b2_r.at[dy], plane(dy, 0)))

    b3 = []

    def along_x():
        for c in b2:
            c.wait_recv()
        for dx in FAR_X + (0,):
            a = request_id(dx, 0)
            from_y = jnp.bitwise_and(jnp.right_shift(a, 4), NY - 1)
            there = jnp.bitwise_and(y - from_y + NY, NY - 1)
            piece = recv2[there, dx]
            if dx == 0:
                recv3[0] = piece
            else:
                send3[dx] = piece
                b3.append(remote(send3.at[dx], recv3.at[dx], b3_s.at[dx], b3_r.at[dx], across(-dx)))

    for dz in (2, 6, 1, 7):
        pass_near(dz)
    load_q.wait()
    angles()
    for c in id_y.values():
        c.wait_recv()
    id_z = {dz: remote(col, ids.at[dz], idz_s.at[dz], idz_r.at[dz], plane(0, dz)) for dz in FAR_Z}
    id_x = [remote(col, xids.at[dx], xid_s.at[dx], xid_r.at[dx], across(dx)) for dx in FAR_X]
    load_a.wait()
    send_group(0)
    pass_on()
    send_group(4)
    send_group(3)
    send_group(5)
    send_group(2)
    send_group(6)
    send_group(1)
    send_group(7)
    along_y()
    attend_heads(0, 2)
    along_x()
    attend_heads(2, 4)

    load_t.wait()

    def token_cols(dy, dz):
        owner = lax.rem(y - dy + NY, NY) * NZ + lax.rem(z - dz + NZ, NZ)
        return tok_v[:, pl.ds(pl.multiple_of((owner * 2 + core) * 128, 128), 128)]

    total = jnp.zeros((ROWS, 2 * RANK), jnp.float32)
    for dz in (0,) + FAR_Z:
        some = [(dy, dz) for dy in FAR_Y + (0,)]
        for o in some:
            if o != (0, 0):
                blocks[slot(*o)].wait_recv()
        left = jnp.concatenate([token_cols(*o) for o in some], axis=1)
        right = jnp.concatenate([recv_a[slot(*o)] for o in some], axis=0)
        total = total + jnp.dot(left, right, preferred_element_type=jnp.float32)
    part[...] = total
    swap = remote(part, part_in, p_s, p_r, sibling)
    for c in b3:
        c.wait_recv()
    swap.wait_recv()
    rank = (part[...] + part_in[...]).astype(jnp.bfloat16)

    alive = lax.broadcasted_iota(jnp.int32, (ROWS, HEAD), 0) < live
    for j in range(2):
        whole = jnp.concatenate([recv3[jnp.bitwise_and(x - req + NX, NX - 1), j] for x in range(NX)], axis=0)
        delta = jnp.dot(rank[:, j * RANK:(j + 1) * RANK], whole, preferred_element_type=jnp.float32)
        fresh = base_v[j].astype(jnp.float32) + delta
        for h in range(KV_HEADS):
            one = fresh[:, h * HEAD:(h + 1) * HEAD]
            if j == 0:
                one = one * angle_v[0] + pltpu.roll(one, HEAD // 2, 1) * angle_v[1]
            new_v[j, :, head_cols(h)] = jnp.where(alive, one, 0.0).astype(jnp.bfloat16)
    new_k[...] = new_v[0]
    new_w[...] = new_v[1]
    outs = (o0, o1, o2, o3, o4, o5, o6, o7)

    column = lax.broadcasted_iota(jnp.int32, (ROWS, HEAD), 1)
    allowed = (column <= row) & (column < live)
    for h in range(KV_HEADS):
        kn = new_v[0, :, head_cols(h)]
        vn = jnp.concatenate([new_v[1, :, head_cols(h)], jnp.ones((ROWS, HEAD), jnp.bfloat16)], axis=1)
        q = jnp.concatenate([q_v[:, head_cols(h * GROUP + i)] for i in range(GROUP)], axis=0)
        s = lax.dot_general(q, kn, (((1,), (1,)), ((), ())), preferred_element_type=jnp.float32)
        s = jnp.where(allowed[None], s.reshape(GROUP, ROWS, HEAD) * SCALE2, LOWEST)
        s = s.reshape(GROUP * ROWS, HEAD)
        r = pl.ds(h * GROUP * ROWS, GROUP * ROWS)
        old = top[r, :]
        m = jnp.maximum(jnp.max(s, axis=1, keepdims=True), old)
        p = jnp.exp2(s - m).astype(jnp.bfloat16)
        o = jnp.dot(p, vn, preferred_element_type=jnp.float32)
        alpha = jnp.exp2(old - m)
        upper = acc[r, :] * alpha + o[:, 0:HEAD]
        lower = alpha + o[:, HEAD:]
        res = upper / lower
        for g in range(GROUP):
            one = jnp.where(alive, res[g * ROWS:(g + 1) * ROWS, :], 0.0)
            outs[2 * h + g // 4][:, head_cols(g % 4)] = one.astype(jnp.bfloat16)
    for c in sends:
        c.wait_send()


def write_out(new_k, new_w, o0, o1, o2, o3, o4, o5, o6, o7, new_out, attn_out, both_v, sem):
    puts = []
    for i, part in enumerate((o0, o1, o2, o3, o4, o5, o6, o7)):
        cols = pl.ds(i * PIECE, PIECE)
        puts.append(pltpu.make_async_copy(part, attn_out.at[:, cols], sem.at[i]))
        puts[-1].start()
    both_v[...] = jnp.stack([new_k[...], new_w[...]], axis=1)
    puts.append(pltpu.make_async_copy(both_v, new_out, sem.at[8]))
    puts[-1].start()
    for c in puts:
        c.wait()


def shards(tokens, queries, plain, cached, first, second, adapter, live, ctx):
    width = plain.shape[2]
    bf16, f32 = jnp.bfloat16, jnp.float32
    dma = pltpu.SemaphoreType.DMA
    smem = pl.BlockSpec(memory_space=pltpu.SMEM)
    hbm = pl.BlockSpec(memory_space=pl.ANY)
    vmem = pl.BlockSpec(memory_space=pltpu.VMEM)
    heads = KV_HEADS * GROUP
    two = (2, ROWS, width)
    pieces = pl.pallas_call(
        kernel,
        out_shape=(jax.ShapeDtypeStruct((ROWS, PIECE), bf16),) * 10,
        in_specs=[smem] * 3 + [hbm] * 6,
        out_specs=(vmem,) * 10,
        scratch_shapes=[
            pltpu.VMEM(tokens.shape, bf16),
            pltpu.VMEM(queries.shape, bf16),
            pltpu.VMEM(plain.shape, bf16),
            pltpu.VMEM(two, bf16),
            pltpu.VMEM((2, CTX, width), bf16),
            pltpu.VMEM(first.shape, bf16),
            pltpu.VMEM((PLANE, 128, 2 * RANK), bf16),
            pltpu.VMEM((PLANE, 128, 2 * RANK), bf16),
            pltpu.VMEM((NZ, 2, 2, 16, width), bf16),
            pltpu.VMEM((NY, NX, 2, 16, width), bf16),
            pltpu.VMEM((NY, NX, 2, 16, width), bf16),
            pltpu.VMEM((NX, 2, 16, width), bf16),
            pltpu.VMEM((NX, 2, 16, width), bf16),
            pltpu.VMEM((ROWS, 2 * RANK), f32),
            pltpu.VMEM((ROWS, 2 * RANK), f32),
            pltpu.VMEM((CTX, HEAD), bf16),
            pltpu.VMEM((CTX, 2 * HEAD), bf16),
            pltpu.VMEM((heads * ROWS, HEAD), f32),
            pltpu.VMEM((heads * ROWS, HEAD), f32),
            pltpu.VMEM((2, ROWS, HEAD), f32),
            pltpu.VMEM(two, bf16),
            pltpu.SMEM((PLANE, 1), jnp.int32),
            pltpu.SMEM((NZ, PLANE, 1), jnp.int32),
            pltpu.SMEM((NX, PLANE, 1), jnp.int32),
            dma((5,)), dma((KV_HEADS,)),
            dma((NY,)), dma((NY,)), dma((NZ,)), dma((NZ,)), dma((NX,)), dma((NX,)),
            dma((PLANE,)), dma((PLANE,)), dma((NZ,)), dma((NZ,)),
            dma((NY,)), dma((NY,)), dma((NX,)), dma((NX,)), dma, dma,
        ],
        compiler_params=pltpu.CompilerParams(
            collective_id=0, has_side_effects=True, vmem_limit_bytes=105 << 19
        ),
    )(adapter, live, ctx, tokens, queries, plain, cached, first, second)
    return pl.pallas_call(
        write_out,
        out_shape=(jax.ShapeDtypeStruct(plain.shape, bf16), jax.ShapeDtypeStruct(queries.shape, bf16)),
        in_specs=[vmem] * 10,
        out_specs=(hbm, hbm),
        scratch_shapes=[pltpu.VMEM(plain.shape, bf16), dma((9,))],
        compiler_params=pltpu.CompilerParams(vmem_limit_bytes=8 << 20),
    )(*pieces)


def solution(mesh):
    in_specs = (
        P(("store", "req"), None),
        P(("store", "req"), "tp"),
        P(("store", "req"), None, "tp"),
        P(("store", "req"), None, None, "tp"),
        P(None, ("store", "tp"), None),
        P("store", None, None, "tp"),
        P(("store", "req")),
        P(("store", "req")),
        P(("store", "req")),
    )
    out_specs = (P(("store", "req"), None, "tp"), P(("store", "req"), "tp"))
    return jax.shard_map(shards, mesh=mesh, in_specs=in_specs, out_specs=out_specs, check_vma=False)
```

```python
import functools
import math

import jax
import jax.numpy as jnp
from jax import lax
from jax.experimental import pallas as pl
from jax.experimental.pallas import tpu as pltpu
from jax.sharding import PartitionSpec as P

HEAD = 128
ROWS = 128
RANK = 64
NY, NZ, NX = 4, 8, 4
PLANE = NY * NZ
GROUP = 8
KV_HEADS = 4
PIECE = 512
CTX = 2048
TILE = 512
SCALE2 = math.log2(math.e) / math.sqrt(HEAD)
LOWEST = -1e30
FAR_X = (2, 1, 3)
FAR_Y = (2, 1, 3)
FAR_Z = (4, 3, 5, 2, 6, 1, 7)
REST = (1, 7, 3, 5, 4, 0)
MESH = pl.DeviceIdType.MESH

def slot(dy, dz):
    return (dy % NY) * NZ + dz % NZ


def head_cols(h):
    return pl.ds(h * HEAD if isinstance(h, int) else pl.multiple_of(h * HEAD, HEAD), HEAD)


def kernel(
    adapter_ref, live_ref, ctx_ref, tokens, queries, plain, cached, first, second,
    new_k, new_w, o0, o1, o2, o3, o4, o5, o6, o7,
    tok_v, q_v, plain_v, base_v, kv_v, first_v, send_a, recv_a, gath, send2, recv2, send3, recv3,
    part, part_in, key_buf, val_buf, acc, top, angle_v, new_v, col, ids, xids,
    lsem, kvsem, idy_s, idy_r, idz_s, idz_r, xid_s, xid_r, a_s, a_r,
    b1_s, b1_r, b2_s, b2_r, b3_s, b3_r, p_s, p_r,
):
    store, req, core = lax.axis_index("store"), lax.axis_index("req"), lax.axis_index("tp")
    y, z = store // NZ, lax.rem(store, NZ)

    def plane(dy, dz):
        return {"store": lax.rem(y + dy % NY, NY) * NZ + lax.rem(z + dz % NZ, NZ)}

    def across(dx):
        return {"req": lax.rem(req + dx % NX, NX)}

    sibling = {"tp": 1 - core}
    sends = []

    def remote(src, dst, s, r, dev):
        c = pltpu.make_async_remote_copy(
            src_ref=src, dst_ref=dst, send_sem=s, recv_sem=r, device_id=dev, device_id_type=MESH
        )
        c.start()
        sends.append(c)
        return c

    bar = pltpu.get_barrier_semaphore()
    peers = [plane(0, dz) for dz in FAR_Z] + [plane(dy, 0) for dy in FAR_Y]
    peers += [across(dx) for dx in FAR_X] + [sibling]
    for dev in peers:
        pl.semaphore_signal(bar, inc=1, device_id=dev, device_id_type=MESH)

    def load(src, dst, i):
        c = pltpu.make_async_copy(src, dst, lsem.at[i])
        c.start()
        return c

    load_q = load(queries, q_v, 0)
    load_kv = []
    for h in range(KV_HEADS):
        c = pltpu.make_async_copy(
            cached.at[0, :, :, head_cols(h)], kv_v.at[:, :, head_cols(h)], kvsem.at[h]
        )
        c.start()
        load_kv.append(c)
        if h == 0:
            load_b = load(second.at[:, :, pl.ds(pl.multiple_of(req * 16, 16), 16), :], gath.at[0], 1)
            load_p = load(plain, plain_v, 3)
            load_a = load(first, first_v, 2)
    load_t = load(tokens, tok_v, 4)

    ctx = ctx_ref[0]
    live = live_ref[0]
    col[0, 0] = adapter_ref[0]

    def attend(h, u):
        per = TILE // ROWS
        g = h * GROUP + u * per
        q = jnp.concatenate([q_v[:, head_cols(g + i)] for i in range(per)], axis=0)
        s = lax.dot_general(
            q, key_buf[...], (((1,), (1,)), ((), ())), preferred_element_type=jnp.float32
        )
        m = jnp.max(s, axis=1, keepdims=True) * SCALE2
        p = jnp.exp2(s * SCALE2 - m).astype(jnp.bfloat16)
        o = jnp.dot(p, val_buf[...], preferred_element_type=jnp.float32)
        lower = jnp.where(ctx > 0, o[:, HEAD:], 1.0)
        r = pl.ds(pl.multiple_of(g * ROWS, ROWS), TILE)
        acc[r, :] = o[:, 0:HEAD] / lower
        top[r, :] = jnp.where(ctx > 0, m + jnp.log2(lower), LOWEST)

    def prepare(h):
        alive = lax.broadcasted_iota(jnp.int32, (CTX, HEAD), 0) < ctx
        k = kv_v[0, :, head_cols(h)]
        v = kv_v[1, :, head_cols(h)]
        key_buf[...] = jnp.where(alive, k, jnp.broadcast_to(k[0:1, :], k.shape))
        val_buf[:, 0:HEAD] = jnp.where(alive, v, jnp.zeros_like(v))
        val_buf[:, HEAD:] = jnp.where(alive, jnp.ones_like(v), jnp.zeros_like(v))

    lane = lax.broadcasted_iota(jnp.int32, (ROWS, HEAD), 1)
    row = lax.broadcasted_iota(jnp.int32, (ROWS, HEAD), 0)

    def attend_heads(lo, hi):
        for c in load_kv[lo:hi]:
            c.wait()

        @pl.loop(lo, hi)
        def _(h):
            prepare(h)
            for u in range(GROUP * ROWS // TILE):
                attend(h, u)

    def angles():
        index = jnp.where(lane < HEAD // 2, lane, lane - HEAD // 2).astype(jnp.float32)
        frequency = jnp.exp(index * (-2.0 / HEAD * math.log(10000.0)))
        angle = (ctx + row).astype(jnp.float32) * frequency
        angle_v[0] = jnp.cos(angle)
        sine = jnp.sin(angle)
        angle_v[1] = jnp.where(lane < HEAD // 2, -sine, sine)
        load_p.wait()
        for j in range(2):
            base_v[j] = plain_v[:, j, :]

    pl.semaphore_wait(bar, len(peers))

    id_y = {dy: remote(adapter_ref, col.at[dy], idy_s.at[dy], idy_r.at[dy], plane(dy, 0)) for dy in FAR_Y}
    load_b.wait()
    near = {}

    def pass_near(dz):
        near[dz] = remote(gath.at[0], gath.at[dz], b1_s.at[dz], b1_r.at[dz], plane(0, dz))

    def pass_on():
        for dz in (2, 6):
            near[dz].wait_recv()
        near[3] = remote(gath.at[2], gath.at[3], b1_s.at[3], b1_r.at[3], plane(0, 1))
        near[5] = remote(gath.at[6], gath.at[5], b1_s.at[5], b1_r.at[5], plane(0, -1))
        near[4] = remote(gath.at[2, 0], gath.at[4, 0], b1_s.at[4], b1_r.at[4], plane(0, 2))
        near[0] = remote(gath.at[6, 1], gath.at[4, 1], b1_s.at[0], b1_r.at[0], plane(0, -2))

    blocks = {}

    def send_block(dy, dz):
        k = slot(dy, dz)
        send_a[k] = first_v[col[-dy % NY, 0] if dz == 0 else ids[-dz % NZ, -dy % NY, 0]]
        blocks[k] = remote(send_a.at[k], recv_a.at[k], a_s.at[k], a_r.at[k], plane(dy, dz))

    def send_group(dz):
        if dz:
            id_z[-dz % NZ].wait_recv()
        else:
            recv_a[0] = first_v[col[0, 0]]
        for dy in FAR_Y + ((0,) if dz else ()):
            send_block(dy, dz)

    def request_id(dx, dy):
        return col[dy % NY, 0] if dx == 0 else xids[dx, dy % NY, 0]

    b2 = []

    def along_y():
        for c in id_x:
            c.wait_recv()
        for dz in REST:
            near[dz].wait_recv()
        for dy in FAR_Y + (0,):
            for dx in range(NX):
                a = request_id(dx, -dy)
                from_z = jnp.bitwise_and(jnp.right_shift(a, 1), NZ - 1)
                there = jnp.bitwise_and(z - from_z + NZ, NZ - 1)
                piece = gath[there, jnp.bitwise_and(a, 1)]
                if dy == 0:
                    recv2[0, dx] = piece
                else:
                    send2[dy, dx] = piece
            if dy:
                b2.append(remote(send2.at[dy], recv2.at[dy], b2_s.at[dy], b2_r.at[dy], plane(dy, 0)))

    b3 = []

    def along_x():
        for c in b2:
            c.wait_recv()
        for dx in FAR_X + (0,):
            a = request_id(dx, 0)
            from_y = jnp.bitwise_and(jnp.right_shift(a, 4), NY - 1)
            there = jnp.bitwise_and(y - from_y + NY, NY - 1)
            piece = recv2[there, dx]
            if dx == 0:
                recv3[0] = piece
            else:
                send3[dx] = piece
                b3.append(remote(send3.at[dx], recv3.at[dx], b3_s.at[dx], b3_r.at[dx], across(-dx)))

    for dz in (2, 6, 1, 7):
        pass_near(dz)
    load_q.wait()
    angles()
    for c in id_y.values():
        c.wait_recv()
    id_z = {dz: remote(col, ids.at[dz], idz_s.at[dz], idz_r.at[dz], plane(0, dz)) for dz in FAR_Z}
    id_x = [remote(col, xids.at[dx], xid_s.at[dx], xid_r.at[dx], across(dx)) for dx in FAR_X]
    load_a.wait()
    send_group(0)
    pass_on()
    send_group(1)
    send_group(7)
    send_group(2)
    send_group(6)
    send_group(3)
    send_group(5)
    send_group(4)
    along_y()
    attend_heads(0, 2)
    along_x()
    attend_heads(2, 4)

    load_t.wait()

    def token_cols(dy, dz):
        owner = lax.rem(y - dy + NY, NY) * NZ + lax.rem(z - dz + NZ, NZ)
        return tok_v[:, pl.ds(pl.multiple_of((owner * 2 + core) * 128, 128), 128)]

    total = jnp.zeros((ROWS, 2 * RANK), jnp.float32)
    for dz in (0,) + FAR_Z:
        some = [(dy, dz) for dy in FAR_Y + (0,)]
        for o in some:
            if o != (0, 0):
                blocks[slot(*o)].wait_recv()
        left = jnp.concatenate([token_cols(*o) for o in some], axis=1)
        right = jnp.concatenate([recv_a[slot(*o)] for o in some], axis=0)
        total = total + jnp.dot(left, right, preferred_element_type=jnp.float32)
    part[...] = total
    swap = remote(part, part_in, p_s, p_r, sibling)
    for c in b3:
        c.wait_recv()
    swap.wait_recv()
    rank = (part[...] + part_in[...]).astype(jnp.bfloat16)

    alive = lax.broadcasted_iota(jnp.int32, (ROWS, HEAD), 0) < live
    for j in range(2):
        whole = jnp.concatenate([recv3[jnp.bitwise_and(x - req + NX, NX - 1), j] for x in range(NX)], axis=0)
        delta = jnp.dot(rank[:, j * RANK:(j + 1) * RANK], whole, preferred_element_type=jnp.float32)
        fresh = base_v[j].astype(jnp.float32) + delta
        for h in range(KV_HEADS):
            one = fresh[:, h * HEAD:(h + 1) * HEAD]
            if j == 0:
                one = one * angle_v[0] + pltpu.roll(one, HEAD // 2, 1) * angle_v[1]
            new_v[j, :, head_cols(h)] = jnp.where(alive, one, 0.0).astype(jnp.bfloat16)
    new_k[...] = new_v[0]
    new_w[...] = new_v[1]
    outs = (o0, o1, o2, o3, o4, o5, o6, o7)

    column = lax.broadcasted_iota(jnp.int32, (ROWS, HEAD), 1)
    allowed = (column <= row) & (column < live)
    for h in range(KV_HEADS):
        kn = new_v[0, :, head_cols(h)]
        vn = jnp.concatenate([new_v[1, :, head_cols(h)], jnp.ones((ROWS, HEAD), jnp.bfloat16)], axis=1)
        q = jnp.concatenate([q_v[:, head_cols(h * GROUP + i)] for i in range(GROUP)], axis=0)
        s = lax.dot_general(q, kn, (((1,), (1,)), ((), ())), preferred_element_type=jnp.float32)
        s = jnp.where(allowed[None], s.reshape(GROUP, ROWS, HEAD) * SCALE2, LOWEST)
        s = s.reshape(GROUP * ROWS, HEAD)
        r = pl.ds(h * GROUP * ROWS, GROUP * ROWS)
        old = top[r, :]
        m = jnp.maximum(jnp.max(s, axis=1, keepdims=True), old)
        p = jnp.exp2(s - m).astype(jnp.bfloat16)
        o = jnp.dot(p, vn, preferred_element_type=jnp.float32)
        alpha = jnp.exp2(old - m)
        upper = acc[r, :] * alpha + o[:, 0:HEAD]
        lower = alpha + o[:, HEAD:]
        res = upper / lower
        for g in range(GROUP):
            one = jnp.where(alive, res[g * ROWS:(g + 1) * ROWS, :], 0.0)
            outs[2 * h + g // 4][:, head_cols(g % 4)] = one.astype(jnp.bfloat16)
    for c in sends:
        c.wait_send()


def write_out(new_k, new_w, o0, o1, o2, o3, o4, o5, o6, o7, new_out, attn_out, both_v, sem):
    puts = []
    for i, part in enumerate((o0, o1, o2, o3, o4, o5, o6, o7)):
        cols = pl.ds(i * PIECE, PIECE)
        puts.append(pltpu.make_async_copy(part, attn_out.at[:, cols], sem.at[i]))
        puts[-1].start()
    both_v[...] = jnp.stack([new_k[...], new_w[...]], axis=1)
    puts.append(pltpu.make_async_copy(both_v, new_out, sem.at[8]))
    puts[-1].start()
    for c in puts:
        c.wait()


def shards(tokens, queries, plain, cached, first, second, adapter, live, ctx):
    width = plain.shape[2]
    bf16, f32 = jnp.bfloat16, jnp.float32
    dma = pltpu.SemaphoreType.DMA
    smem = pl.BlockSpec(memory_space=pltpu.SMEM)
    hbm = pl.BlockSpec(memory_space=pl.ANY)
    vmem = pl.BlockSpec(memory_space=pltpu.VMEM)
    heads = KV_HEADS * GROUP
    two = (2, ROWS, width)
    pieces = pl.pallas_call(
        kernel,
        out_shape=(jax.ShapeDtypeStruct((ROWS, PIECE), bf16),) * 10,
        in_specs=[smem] * 3 + [hbm] * 6,
        out_specs=(vmem,) * 10,
        scratch_shapes=[
            pltpu.VMEM(tokens.shape, bf16),
            pltpu.VMEM(queries.shape, bf16),
            pltpu.VMEM(plain.shape, bf16),
            pltpu.VMEM(two, bf16),
            pltpu.VMEM((2, CTX, width), bf16),
            pltpu.VMEM(first.shape, bf16),
            pltpu.VMEM((PLANE, 128, 2 * RANK), bf16),
            pltpu.VMEM((PLANE, 128, 2 * RANK), bf16),
            pltpu.VMEM((NZ, 2, 2, 16, width), bf16),
            pltpu.VMEM((NY, NX, 2, 16, width), bf16),
            pltpu.VMEM((NY, NX, 2, 16, width), bf16),
            pltpu.VMEM((NX, 2, 16, width), bf16),
            pltpu.VMEM((NX, 2, 16, width), bf16),
            pltpu.VMEM((ROWS, 2 * RANK), f32),
            pltpu.VMEM((ROWS, 2 * RANK), f32),
            pltpu.VMEM((CTX, HEAD), bf16),
            pltpu.VMEM((CTX, 2 * HEAD), bf16),
            pltpu.VMEM((heads * ROWS, HEAD), f32),
            pltpu.VMEM((heads * ROWS, HEAD), f32),
            pltpu.VMEM((2, ROWS, HEAD), f32),
            pltpu.VMEM(two, bf16),
            pltpu.SMEM((PLANE, 1), jnp.int32),
            pltpu.SMEM((NZ, PLANE, 1), jnp.int32),
            pltpu.SMEM((NX, PLANE, 1), jnp.int32),
            dma((5,)), dma((KV_HEADS,)),
            dma((NY,)), dma((NY,)), dma((NZ,)), dma((NZ,)), dma((NX,)), dma((NX,)),
            dma((PLANE,)), dma((PLANE,)), dma((NZ,)), dma((NZ,)),
            dma((NY,)), dma((NY,)), dma((NX,)), dma((NX,)), dma, dma,
        ],
        compiler_params=pltpu.CompilerParams(
            collective_id=0, has_side_effects=True, vmem_limit_bytes=105 << 19
        ),
    )(adapter, live, ctx, tokens, queries, plain, cached, first, second)
    return pl.pallas_call(
        write_out,
        out_shape=(jax.ShapeDtypeStruct(plain.shape, bf16), jax.ShapeDtypeStruct(queries.shape, bf16)),
        in_specs=[vmem] * 10,
        out_specs=(hbm, hbm),
        scratch_shapes=[pltpu.VMEM(plain.shape, bf16), dma((9,))],
        compiler_params=pltpu.CompilerParams(vmem_limit_bytes=8 << 20),
    )(*pieces)


def solution(mesh):
    in_specs = (
        P(("store", "req"), None),
        P(("store", "req"), "tp"),
        P(("store", "req"), None, "tp"),
        P(("store", "req"), None, None, "tp"),
        P(None, ("store", "tp"), None),
        P("store", None, None, "tp"),
        P(("store", "req")),
        P(("store", "req")),
        P(("store", "req")),
    )
    out_specs = (P(("store", "req"), None, "tp"), P(("store", "req"), "tp"))
    return jax.shard_map(shards, mesh=mesh, in_specs=in_specs, out_specs=out_specs, check_vma=False)
```

```python
import functools
import math

import jax
import jax.numpy as jnp
from jax import lax
from jax.experimental import pallas as pl
from jax.experimental.pallas import tpu as pltpu
from jax.sharding import PartitionSpec as P

HEAD = 128
ROWS = 128
RANK = 64
NY, NZ, NX = 4, 8, 4
PLANE = NY * NZ
GROUP = 8
KV_HEADS = 4
PIECE = 512
CTX = 2048
TILE = 512
SCALE2 = math.log2(math.e) / math.sqrt(HEAD)
LOWEST = -1e30
FAR_X = (2, 1, 3)
FAR_Y = (2, 1, 3)
FAR_Z = (4, 3, 5, 2, 6, 1, 7)
NEAR_Z = (1, 7, 2, 6, 3, 5, 4)
REST = (1, 7, 3, 5, 4, 0)
MESH = pl.DeviceIdType.MESH

def slot(dy, dz):
    return (dy % NY) * NZ + dz % NZ


def head_cols(h):
    return pl.ds(h * HEAD if isinstance(h, int) else pl.multiple_of(h * HEAD, HEAD), HEAD)


def kernel(
    adapter_ref, live_ref, ctx_ref, tokens, queries, plain, cached, first, second,
    new_k, new_w, o0, o1, o2, o3, o4, o5, o6, o7,
    tok_v, q_v, plain_v, base_v, kv_v, first_v, send_a, recv_a, gath, send2, recv2, send3, recv3,
    part, part_in, key_buf, val_buf, acc, top, angle_v, new_v, col, ids, xids,
    lsem, kvsem, idy_s, idy_r, idz_s, idz_r, xid_s, xid_r, a_s, a_r,
    b1_s, b1_r, b2_s, b2_r, b3_s, b3_r, p_s, p_r,
):
    store, req, core = lax.axis_index("store"), lax.axis_index("req"), lax.axis_index("tp")
    y, z = store // NZ, lax.rem(store, NZ)

    def plane(dy, dz):
        return {"store": lax.rem(y + dy % NY, NY) * NZ + lax.rem(z + dz % NZ, NZ)}

    def across(dx):
        return {"req": lax.rem(req + dx % NX, NX)}

    sibling = {"tp": 1 - core}
    sends = []

    def remote(src, dst, s, r, dev):
        c = pltpu.make_async_remote_copy(
            src_ref=src, dst_ref=dst, send_sem=s, recv_sem=r, device_id=dev, device_id_type=MESH
        )
        c.start()
        sends.append(c)
        return c

    bar = pltpu.get_barrier_semaphore()
    peers = [plane(0, dz) for dz in FAR_Z] + [plane(dy, 0) for dy in FAR_Y]
    peers += [across(dx) for dx in FAR_X] + [sibling]
    for dev in peers:
        pl.semaphore_signal(bar, inc=1, device_id=dev, device_id_type=MESH)

    def load(src, dst, i):
        c = pltpu.make_async_copy(src, dst, lsem.at[i])
        c.start()
        return c

    load_q = load(queries, q_v, 0)
    load_kv = []
    for h in range(KV_HEADS):
        c = pltpu.make_async_copy(
            cached.at[0, :, :, head_cols(h)], kv_v.at[:, :, head_cols(h)], kvsem.at[h]
        )
        c.start()
        load_kv.append(c)
        if h == 0:
            load_b = load(second.at[:, :, pl.ds(pl.multiple_of(req * 16, 16), 16), :], gath.at[0], 1)
            load_p = load(plain, plain_v, 3)
            load_a = load(first, first_v, 2)
    load_t = load(tokens, tok_v, 4)

    ctx = ctx_ref[0]
    live = live_ref[0]
    col[0, 0] = adapter_ref[0]

    def attend(h, u):
        per = TILE // ROWS
        g = h * GROUP + u * per
        q = jnp.concatenate([q_v[:, head_cols(g + i)] for i in range(per)], axis=0)
        s = lax.dot_general(
            q, key_buf[...], (((1,), (1,)), ((), ())), preferred_element_type=jnp.float32
        )
        m = jnp.max(s, axis=1, keepdims=True) * SCALE2
        p = jnp.exp2(s * SCALE2 - m).astype(jnp.bfloat16)
        o = jnp.dot(p, val_buf[...], preferred_element_type=jnp.float32)
        lower = jnp.where(ctx > 0, o[:, HEAD:], 1.0)
        r = pl.ds(pl.multiple_of(g * ROWS, ROWS), TILE)
        acc[r, :] = o[:, 0:HEAD] / lower
        top[r, :] = jnp.where(ctx > 0, m + jnp.log2(lower), LOWEST)

    def prepare(h):
        alive = lax.broadcasted_iota(jnp.int32, (CTX, HEAD), 0) < ctx
        k = kv_v[0, :, head_cols(h)]
        v = kv_v[1, :, head_cols(h)]
        key_buf[...] = jnp.where(alive, k, jnp.broadcast_to(k[0:1, :], k.shape))
        val_buf[:, 0:HEAD] = jnp.where(alive, v, jnp.zeros_like(v))
        val_buf[:, HEAD:] = jnp.where(alive, jnp.ones_like(v), jnp.zeros_like(v))

    lane = lax.broadcasted_iota(jnp.int32, (ROWS, HEAD), 1)
    row = lax.broadcasted_iota(jnp.int32, (ROWS, HEAD), 0)

    def attend_heads(lo, hi):
        for c in load_kv[lo:hi]:
            c.wait()

        @pl.loop(lo, hi)
        def _(h):
            prepare(h)
            for u in range(GROUP * ROWS // TILE):
                attend(h, u)

    def angles():
        index = jnp.where(lane < HEAD // 2, lane, lane - HEAD // 2).astype(jnp.float32)
        frequency = jnp.exp(index * (-2.0 / HEAD * math.log(10000.0)))
        angle = (ctx + row).astype(jnp.float32) * frequency
        angle_v[0] = jnp.cos(angle)
        sine = jnp.sin(angle)
        angle_v[1] = jnp.where(lane < HEAD // 2, -sine, sine)
        load_p.wait()
        for j in range(2):
            base_v[j] = plain_v[:, j, :]

    pl.semaphore_wait(bar, len(peers))

    id_y = {dy: remote(adapter_ref, col.at[dy], idy_s.at[dy], idy_r.at[dy], plane(dy, 0)) for dy in FAR_Y}
    load_b.wait()
    near = {}

    def pass_near(dz):
        near[dz] = remote(gath.at[0], gath.at[dz], b1_s.at[dz], b1_r.at[dz], plane(0, dz))

    def pass_on():
        for dz in (2, 6):
            near[dz].wait_recv()
        near[3] = remote(gath.at[2], gath.at[3], b1_s.at[3], b1_r.at[3], plane(0, 1))
        near[5] = remote(gath.at[6], gath.at[5], b1_s.at[5], b1_r.at[5], plane(0, -1))
        near[4] = remote(gath.at[2, 0], gath.at[4, 0], b1_s.at[4], b1_r.at[4], plane(0, 2))
        near[0] = remote(gath.at[6, 1], gath.at[4, 1], b1_s.at[0], b1_r.at[0], plane(0, -2))

    blocks = {}

    def send_block(dy, dz):
        k = slot(dy, dz)
        send_a[k] = first_v[col[-dy % NY, 0] if dz == 0 else ids[-dz % NZ, -dy % NY, 0]]
        blocks[k] = remote(send_a.at[k], recv_a.at[k], a_s.at[k], a_r.at[k], plane(dy, dz))

    def send_group(dz):
        if dz:
            id_z[-dz % NZ].wait_recv()
        else:
            recv_a[0] = first_v[col[0, 0]]
        for dy in FAR_Y + ((0,) if dz else ()):
            send_block(dy, dz)

    def request_id(dx, dy):
        return col[dy % NY, 0] if dx == 0 else xids[dx, dy % NY, 0]

    b2 = []

    def along_y():
        for c in id_x:
            c.wait_recv()
        for dz in REST:
            near[dz].wait_recv()
        for dy in FAR_Y + (0,):
            for dx in range(NX):
                a = request_id(dx, -dy)
                from_z = jnp.bitwise_and(jnp.right_shift(a, 1), NZ - 1)
                there = jnp.bitwise_and(z - from_z + NZ, NZ - 1)
                piece = gath[there, jnp.bitwise_and(a, 1)]
                if dy == 0:
                    recv2[0, dx] = piece
                else:
                    send2[dy, dx] = piece
            if dy:
                b2.append(remote(send2.at[dy], recv2.at[dy], b2_s.at[dy], b2_r.at[dy], plane(dy, 0)))

    b3 = []

    def along_x():
        for c in b2:
            c.wait_recv()
        for dx in FAR_X + (0,):
            a = request_id(dx, 0)
            from_y = jnp.bitwise_and(jnp.right_shift(a, 4), NY - 1)
            there = jnp.bitwise_and(y - from_y + NY, NY - 1)
            piece = recv2[there, dx]
            if dx == 0:
                recv3[0] = piece
            else:
                send3[dx] = piece
                b3.append(remote(send3.at[dx], recv3.at[dx], b3_s.at[dx], b3_r.at[dx], across(-dx)))

    for dz in (2, 6, 1, 7):
        pass_near(dz)
    load_q.wait()
    angles()
    for c in id_y.values():
        c.wait_recv()
    id_z = {dz: remote(col, ids.at[dz], idz_s.at[dz], idz_r.at[dz], plane(0, dz)) for dz in FAR_Z}
    id_x = [remote(col, xids.at[dx], xid_s.at[dx], xid_r.at[dx], across(dx)) for dx in FAR_X]
    load_a.wait()
    send_group(0)
    pass_on()
    for dz in NEAR_Z:
        send_group(dz)
    along_y()
    attend_heads(0, 2)
    along_x()
    attend_heads(2, 4)

    load_t.wait()

    def token_cols(dy, dz):
        owner = lax.rem(y - dy + NY, NY) * NZ + lax.rem(z - dz + NZ, NZ)
        return tok_v[:, pl.ds(pl.multiple_of((owner * 2 + core) * 128, 128), 128)]

    total = jnp.zeros((ROWS, 2 * RANK), jnp.float32)
    for dz in (0,) + NEAR_Z:
        some = [(dy, dz) for dy in FAR_Y + (0,)]
        for o in some:
            if o != (0, 0):
                blocks[slot(*o)].wait_recv()
        left = jnp.concatenate([token_cols(*o) for o in some], axis=1)
        right = jnp.concatenate([recv_a[slot(*o)] for o in some], axis=0)
        total = total + jnp.dot(left, right, preferred_element_type=jnp.float32)
    part[...] = total
    swap = remote(part, part_in, p_s, p_r, sibling)
    for c in b3:
        c.wait_recv()
    swap.wait_recv()
    rank = (part[...] + part_in[...]).astype(jnp.bfloat16)

    alive = lax.broadcasted_iota(jnp.int32, (ROWS, HEAD), 0) < live
    for j in range(2):
        whole = jnp.concatenate([recv3[jnp.bitwise_and(x - req + NX, NX - 1), j] for x in range(NX)], axis=0)
        delta = jnp.dot(rank[:, j * RANK:(j + 1) * RANK], whole, preferred_element_type=jnp.float32)
        fresh = base_v[j].astype(jnp.float32) + delta
        for h in range(KV_HEADS):
            one = fresh[:, h * HEAD:(h + 1) * HEAD]
            if j == 0:
                one = one * angle_v[0] + pltpu.roll(one, HEAD // 2, 1) * angle_v[1]
            new_v[j, :, head_cols(h)] = jnp.where(alive, one, 0.0).astype(jnp.bfloat16)
    new_k[...] = new_v[0]
    new_w[...] = new_v[1]
    outs = (o0, o1, o2, o3, o4, o5, o6, o7)

    column = lax.broadcasted_iota(jnp.int32, (ROWS, HEAD), 1)
    allowed = (column <= row) & (column < live)
    for h in range(KV_HEADS):
        kn = new_v[0, :, head_cols(h)]
        vn = jnp.concatenate([new_v[1, :, head_cols(h)], jnp.ones((ROWS, HEAD), jnp.bfloat16)], axis=1)
        q = jnp.concatenate([q_v[:, head_cols(h * GROUP + i)] for i in range(GROUP)], axis=0)
        s = lax.dot_general(q, kn, (((1,), (1,)), ((), ())), preferred_element_type=jnp.float32)
        s = jnp.where(allowed[None], s.reshape(GROUP, ROWS, HEAD) * SCALE2, LOWEST)
        s = s.reshape(GROUP * ROWS, HEAD)
        r = pl.ds(h * GROUP * ROWS, GROUP * ROWS)
        old = top[r, :]
        m = jnp.maximum(jnp.max(s, axis=1, keepdims=True), old)
        p = jnp.exp2(s - m).astype(jnp.bfloat16)
        o = jnp.dot(p, vn, preferred_element_type=jnp.float32)
        alpha = jnp.exp2(old - m)
        upper = acc[r, :] * alpha + o[:, 0:HEAD]
        lower = alpha + o[:, HEAD:]
        res = upper / lower
        for g in range(GROUP):
            one = jnp.where(alive, res[g * ROWS:(g + 1) * ROWS, :], 0.0)
            outs[2 * h + g // 4][:, head_cols(g % 4)] = one.astype(jnp.bfloat16)
    for c in sends:
        c.wait_send()


def write_out(new_k, new_w, o0, o1, o2, o3, o4, o5, o6, o7, new_out, attn_out, both_v, sem):
    puts = []
    for i, part in enumerate((o0, o1, o2, o3, o4, o5, o6, o7)):
        cols = pl.ds(i * PIECE, PIECE)
        puts.append(pltpu.make_async_copy(part, attn_out.at[:, cols], sem.at[i]))
        puts[-1].start()
    both_v[...] = jnp.stack([new_k[...], new_w[...]], axis=1)
    puts.append(pltpu.make_async_copy(both_v, new_out, sem.at[8]))
    puts[-1].start()
    for c in puts:
        c.wait()


def shards(tokens, queries, plain, cached, first, second, adapter, live, ctx):
    width = plain.shape[2]
    bf16, f32 = jnp.bfloat16, jnp.float32
    dma = pltpu.SemaphoreType.DMA
    smem = pl.BlockSpec(memory_space=pltpu.SMEM)
    hbm = pl.BlockSpec(memory_space=pl.ANY)
    vmem = pl.BlockSpec(memory_space=pltpu.VMEM)
    heads = KV_HEADS * GROUP
    two = (2, ROWS, width)
    pieces = pl.pallas_call(
        kernel,
        out_shape=(jax.ShapeDtypeStruct((ROWS, PIECE), bf16),) * 10,
        in_specs=[smem] * 3 + [hbm] * 6,
        out_specs=(vmem,) * 10,
        scratch_shapes=[
            pltpu.VMEM(tokens.shape, bf16),
            pltpu.VMEM(queries.shape, bf16),
            pltpu.VMEM(plain.shape, bf16),
            pltpu.VMEM(two, bf16),
            pltpu.VMEM((2, CTX, width), bf16),
            pltpu.VMEM(first.shape, bf16),
            pltpu.VMEM((PLANE, 128, 2 * RANK), bf16),
            pltpu.VMEM((PLANE, 128, 2 * RANK), bf16),
            pltpu.VMEM((NZ, 2, 2, 16, width), bf16),
            pltpu.VMEM((NY, NX, 2, 16, width), bf16),
            pltpu.VMEM((NY, NX, 2, 16, width), bf16),
            pltpu.VMEM((NX, 2, 16, width), bf16),
            pltpu.VMEM((NX, 2, 16, width), bf16),
            pltpu.VMEM((ROWS, 2 * RANK), f32),
            pltpu.VMEM((ROWS, 2 * RANK), f32),
            pltpu.VMEM((CTX, HEAD), bf16),
            pltpu.VMEM((CTX, 2 * HEAD), bf16),
            pltpu.VMEM((heads * ROWS, HEAD), f32),
            pltpu.VMEM((heads * ROWS, HEAD), f32),
            pltpu.VMEM((2, ROWS, HEAD), f32),
            pltpu.VMEM(two, bf16),
            pltpu.SMEM((PLANE, 1), jnp.int32),
            pltpu.SMEM((NZ, PLANE, 1), jnp.int32),
            pltpu.SMEM((NX, PLANE, 1), jnp.int32),
            dma((5,)), dma((KV_HEADS,)),
            dma((NY,)), dma((NY,)), dma((NZ,)), dma((NZ,)), dma((NX,)), dma((NX,)),
            dma((PLANE,)), dma((PLANE,)), dma((NZ,)), dma((NZ,)),
            dma((NY,)), dma((NY,)), dma((NX,)), dma((NX,)), dma, dma,
        ],
        compiler_params=pltpu.CompilerParams(
            collective_id=0, has_side_effects=True, vmem_limit_bytes=105 << 19
        ),
    )(adapter, live, ctx, tokens, queries, plain, cached, first, second)
    return pl.pallas_call(
        write_out,
        out_shape=(jax.ShapeDtypeStruct(plain.shape, bf16), jax.ShapeDtypeStruct(queries.shape, bf16)),
        in_specs=[vmem] * 10,
        out_specs=(hbm, hbm),
        scratch_shapes=[pltpu.VMEM(plain.shape, bf16), dma((9,))],
        compiler_params=pltpu.CompilerParams(vmem_limit_bytes=8 << 20),
    )(*pieces)


def solution(mesh):
    in_specs = (
        P(("store", "req"), None),
        P(("store", "req"), "tp"),
        P(("store", "req"), None, "tp"),
        P(("store", "req"), None, None, "tp"),
        P(None, ("store", "tp"), None),
        P("store", None, None, "tp"),
        P(("store", "req")),
        P(("store", "req")),
        P(("store", "req")),
    )
    out_specs = (P(("store", "req"), None, "tp"), P(("store", "req"), "tp"))
    return jax.shard_map(shards, mesh=mesh, in_specs=in_specs, out_specs=out_specs, check_vma=False)
```
